32 devices in a mesh: groups: 2 (over x), member: 16 (over z, y, core).
Axes of the slice: x: 2, y: 2, z: 4, core: 2. Of those that a mesh axis runs over, the one named last changes fastest.
Arguments:
- tile_values: bfloat16 [32, 64, 4, 128, 128], P(('groups', 'member')), parts along dimension 0, may hold values from -0.25 to 0.25
- directions: bfloat16 [32, 24, 8192], P(('groups', 'member')), parts along dimension 0, may hold values from -6 to 6
- columns: int32 [64, 4], replicated, may hold values from 0 to 63
- counts: int32 [64], replicated, may hold values from 1 to 4, as said below
- weights: float32 [8192], replicated, may hold values from 2.4414063e-05 to 0.00024414062
Outputs:
- gram_rows: float32 [768, 384], P(('groups', 'member')), parts along dimension 0
The draws below stay inside these ranges and needn't reach their ends.
There are 2 independent parts, one for each index of `groups`. The reference program is written for one: setup_inputs(seed, part) draws one part's arguments, and reference() takes and returns one part's arrays. A program takes and returns all parts, laid end to end along the dimension named above; an argument that names none is the same for every part. Nothing has to cross between parts.
Inputs may be any that keep to these rules, and one draw needn't show every extreme that they name: `counts`: some row tile has all 4 slots live.
All inputs are finite; a program needn't handle non-finite values.
Results may differ from the reference program's by a relative error of at most 0.0013.
Values may be sent and summed in bfloat16 or wider, within the bound.
A program may use at most 64 MiB of HBM per device.

```python
import math
import jax
import jax.numpy as jnp
from jax import lax

B = 128
RT = 64
TPR = 4
S = 24
ROWS = 8192
MEMBERS = 16


def draw_counts(key, part):
    key = jax.random.fold_in(key, 3)
    first_key, second_key = jax.random.split(key)
    values = jax.random.randint(first_key, (RT,), 1, TPR + 1)
    chosen = jax.random.randint(second_key, (), 0, RT)
    positions = jnp.arange(RT)
    return jnp.where(positions == chosen, TPR, values).astype(jnp.int32)


def with_ends(array, key, smallest, top_value):
    spot = [jax.random.randint(jax.random.fold_in(key, axis), (), 0, length) for axis, length in enumerate(array.shape)]
    longest = array.shape.index(max(array.shape))
    next_to = spot[:longest] + [(spot[longest] + 1) % array.shape[longest]] + spot[longest + 1:]
    return array.at[tuple(spot)].set(smallest).at[tuple(next_to)].set(top_value)


def block_scale(stream_key, shape, shards, low, top_value):
    level = 1.0
    for position, parts in shards:
        heights = jax.random.uniform(jax.random.fold_in(jax.random.fold_in(stream_key, 6), position), (parts,), jnp.float32, low / len(shards), top_value / len(shards))
        level = level * jnp.repeat(jnp.exp(heights), shape[position] // parts).reshape((-1,) + (1,) * (len(shape) - 1 - position))
    return level


def gaussian(rng, extent, deviation, limit, cuts=(), dtype=jnp.bfloat16):
    gain = block_scale(rng, extent, cuts, -0.22, 0.18) if cuts else 1.0
    drawn = jax.random.normal(rng, extent, jnp.float32) * deviation * gain
    return jnp.minimum(jnp.maximum(drawn, -limit), limit).astype(dtype)


def setup_inputs(seed: int = 0, part: int = 0) -> dict:
    arg_keys = jax.random.split(jax.random.key(seed), 6)
    part_splits = jax.random.split(jax.random.fold_in(arg_keys[5], part), 6)
    tile_values = gaussian(part_splits[0], (MEMBERS, RT, TPR, B, B), (TPR * B) ** -0.5, 0.25, ((0, 16),))
    directions = gaussian(part_splits[1], (MEMBERS, S, ROWS), 1.0, 6.0, ((0, 16),))
    columns = with_ends(jax.random.randint(arg_keys[2], (RT, TPR), 0, RT), jax.random.fold_in(arg_keys[2], 1), 0, RT - 1).astype(jnp.int32)
    counts = draw_counts(jax.random.fold_in(arg_keys[5], 71), part)
    weights = jnp.clip(jnp.exp(jax.random.uniform(arg_keys[4], (ROWS,), jnp.float32, math.log(2.441406286379788e-05), math.log(0.00024414062))), 2.441406286379788e-05, 0.00024414062)
    return {"tile_values": tile_values, "directions": directions, "columns": columns, "counts": counts, "weights": weights}


def member_snapshot(inputs, columns, counts):
    tiles_one, dirs_one = inputs
    row_tiles, per_row, tile_size, _ = tiles_one.shape
    snaps = dirs_one.shape[0]
    blocks = dirs_one.reshape(snaps, row_tiles, tile_size)
    picked = blocks[:, columns, :]
    slot_ids = lax.broadcasted_iota(jnp.int32, (row_tiles, per_row), 1)
    live_mask = (slot_ids < counts[:, None]).astype(jnp.bfloat16)
    picked = picked * live_mask[None, :, :, None]
    result = jnp.einsum("rkij,srkj->sri", tiles_one.astype(jnp.float32), picked.astype(jnp.float32))
    return result.reshape(snaps, row_tiles * tile_size).astype(jnp.bfloat16)


def reference(tile_values, directions, columns, counts, weights):
    snapshots = lax.map(lambda inputs: member_snapshot(inputs, columns, counts), (tile_values, directions))
    flat = snapshots.reshape(-1, snapshots.shape[2])
    weighted = (flat.astype(jnp.float32) * weights[None, :]).astype(jnp.bfloat16)
    return lax.dot_general(weighted, flat, (((1,), (1,)), ((), ())), preferred_element_type=jnp.float32)
```

```python
import functools

import jax
import jax.numpy as jnp
from jax import lax
from jax.experimental import pallas as pl
from jax.experimental.pallas import tpu as pltpu
from jax.sharding import PartitionSpec as P

MESH = pl.DeviceIdType.MESH
LANES = 128


def kernel(n, fold, tiles_hbm, dirs_ref, cols_ref, counts_ref, weights_ref, out_ref,
           tiles, dirs, snap_out, snap_in, gram, gram_out, gram_in,
           tile_sem, send1, recv1, send2, recv2):
    me = lax.axis_index("member")
    row_tiles, per_row = cols_ref.shape
    snaps = dirs_ref.shape[1]
    chunk = row_tiles // n
    half = n // 2
    strips = n * snaps // LANES

    def nth(step):
        off = half + (step % 2) * ((step + 1) // 2) - ((step + 1) % 2) * (step // 2)
        return lax.rem(me + off, n)

    def tile_copy(step):
        rows = pl.ds(nth(step) * chunk, chunk)
        return pltpu.make_async_copy(tiles_hbm.at[0, rows], tiles.at[rows], tile_sem.at[step])

    def snap_copy(dest, source):
        return pltpu.make_async_remote_copy(
            src_ref=snap_out.at[dest], dst_ref=snap_in.at[source],
            send_sem=send1.at[dest], recv_sem=recv1.at[source],
            device_id={"member": dest}, device_id_type=MESH)

    def gram_copy(dest, source):
        return pltpu.make_async_remote_copy(
            src_ref=gram_out.at[dest], dst_ref=gram_in.at[source],
            send_sem=send2.at[dest], recv_sem=recv2.at[source],
            device_id={"member": dest}, device_id_type=MESH)

    def start_tiles(step, carry):
        tile_copy(step).start()
        return carry

    lax.fori_loop(0, n, start_tiles, 0)

    barrier = pltpu.get_barrier_semaphore()

    def greet(off, carry):
        pl.semaphore_signal(barrier, inc=1, device_id={"member": lax.rem(me + off, n)},
                            device_id_type=MESH)
        return carry

    lax.fori_loop(1, n, greet, 0)

    for c in range(row_tiles):
        dirs[c] = dirs_ref[0, :, c * LANES:(c + 1) * LANES]
    dirs[row_tiles] = jnp.zeros(dirs.shape[1:], dirs.dtype)

    def product(dest):
        parts = []
        for t in range(chunk):
            r = dest * chunk + t
            picked = []
            for k in range(per_row):
                picked.append(dirs[jnp.where(k < counts_ref[r], cols_ref[r, k], row_tiles)])
            lhs = jnp.concatenate(picked, axis=1)
            rhs = jnp.concatenate([tiles[r, k] for k in range(per_row)], axis=1)
            parts.append(lax.dot_general(lhs, rhs, (((1,), (1,)), ((), ())),
                                         preferred_element_type=jnp.float32))
        each = chunk // fold
        rows = [jnp.concatenate(parts[f * each:(f + 1) * each], axis=1) for f in range(fold)]
        return jnp.concatenate(rows, axis=0).astype(jnp.bfloat16)

    def one(step):
        tile_copy(step).wait()
        dest = nth(step)
        snap_out[dest] = product(dest)
        snap_copy(dest, me).start()

    tile_copy(0).wait()
    first = nth(0)
    snap_out[first] = product(first)
    pl.semaphore_wait(barrier, n - 1)
    snap_copy(first, me).start()

    def body(step, carry):
        one(step)
        return carry

    lax.fori_loop(1, n - 1, body, 0)
    tile_copy(n - 1).wait()
    snap_in[me] = product(me)

    def land(step, carry):
        snap_copy(me, nth(step)).wait_recv()
        return carry

    lax.fori_loop(0, n - 1, land, 0)

    each = chunk // fold
    flats, weighteds = [], []
    for f in range(fold):
        for t in range(each):
            got = snap_in[:, :, t * LANES:(t + 1) * LANES].astype(jnp.float32)
            flat = got[:, f * snaps:(f + 1) * snaps].reshape(n * snaps, LANES)
            w = weights_ref[pl.ds(me * chunk + f * each + t, 1), :]
            flats.append(flat.astype(jnp.bfloat16))
            weighteds.append((flat * w).astype(jnp.bfloat16))
    total = lax.dot_general(jnp.concatenate(weighteds, axis=1), jnp.concatenate(flats, axis=1),
                            (((1,), (1,)), ((), ())), preferred_element_type=jnp.float32)
    gram[...] = total.reshape(n, snaps, n * snaps)

    def give(step, carry):
        dest = nth(step)
        block = gram[dest]
        gram_out[dest] = jnp.concatenate(
            [block[:, c * LANES:(c + 1) * LANES] for c in range(strips)], axis=0
        ).astype(jnp.bfloat16)
        gram_copy(dest, me).start()
        return carry

    lax.fori_loop(0, n - 1, give, 0)
    out_ref[...] = gram[me]

    def take(step, carry):
        source = nth(step)
        gram_copy(me, source).wait_recv()
        got = gram_in[source].astype(jnp.float32)
        out_ref[...] += jnp.concatenate(
            [got[c * snaps:(c + 1) * snaps] for c in range(strips)], axis=1)
        return carry

    lax.fori_loop(0, n - 1, take, 0)

    def drain(step, carry):
        snap_copy(nth(step), me).wait_send()
        gram_copy(nth(step), me).wait_send()
        return carry

    lax.fori_loop(0, n - 1, drain, 0)


def per_device(n, tile_values, directions, columns, counts, weights):
    _, row_tiles, per_row, size, _ = tile_values.shape
    snaps = directions.shape[1]
    chunk = row_tiles // n
    fold = 2 if chunk % 2 == 0 else 1
    strips = n * snaps // LANES
    message = (n, fold * snaps, chunk * size // fold)
    block = (n, strips * snaps, LANES)
    vmem = pl.BlockSpec(memory_space=pltpu.VMEM)
    smem = pl.BlockSpec(memory_space=pltpu.SMEM)
    return pl.pallas_call(
        functools.partial(kernel, n, fold),
        out_shape=jax.ShapeDtypeStruct((snaps, n * snaps), jnp.float32),
        in_specs=[pl.BlockSpec(memory_space=pl.ANY), vmem, smem, smem, vmem],
        out_specs=vmem,
        scratch_shapes=[
            pltpu.VMEM((row_tiles, per_row, size, size), jnp.bfloat16),
            pltpu.VMEM((row_tiles + 1, snaps, size), jnp.bfloat16),
            pltpu.VMEM(message, jnp.bfloat16),
            pltpu.VMEM(message, jnp.bfloat16),
            pltpu.VMEM((n, snaps, n * snaps), jnp.float32),
            pltpu.VMEM(block, jnp.bfloat16),
            pltpu.VMEM(block, jnp.bfloat16),
            pltpu.SemaphoreType.DMA((n,)),
            pltpu.SemaphoreType.DMA((n,)),
            pltpu.SemaphoreType.DMA((n,)),
            pltpu.SemaphoreType.DMA((n,)),
            pltpu.SemaphoreType.DMA((n,)),
        ],
        compiler_params=pltpu.CompilerParams(
            collective_id=0, has_side_effects=True, vmem_limit_bytes=48 * 2**20),
    )(tile_values, directions, columns, counts, weights.reshape(-1, LANES))


def solution(mesh):
    in_specs = (
        P(("groups", "member"), None, None, None, None),
        P(("groups", "member"), None, None),
        P(),
        P(),
        P(),
    )
    out_specs = P(("groups", "member"), None)
    return jax.shard_map(
        functools.partial(per_device, mesh.shape["member"]), mesh=mesh,
        in_specs=in_specs, out_specs=out_specs, check_vma=False
    )
```

```python
import functools

import jax
import jax.numpy as jnp
from jax import lax
from jax.experimental import pallas as pl
from jax.experimental.pallas import tpu as pltpu
from jax.sharding import PartitionSpec as P

MESH = pl.DeviceIdType.MESH
LANES = 128


def pack(block):
    snaps, columns = block.shape
    full = columns // LANES
    rows = [block[:, c * LANES:(c + 1) * LANES] for c in range(full)]
    if columns % LANES:
        rest = block[:, full * LANES:]
        left = rest[:16]
        right = jnp.concatenate([rest[16:], jnp.zeros((32 - snaps, LANES // 2), rest.dtype)], axis=0)
        rows.append(jnp.concatenate([left, right], axis=1))
    return jnp.concatenate(rows, axis=0)


def unpack(rows, snaps, columns):
    full = columns // LANES
    parts = [rows[c * snaps:(c + 1) * snaps] for c in range(full)]
    if columns % LANES:
        rest = rows[full * snaps:]
        parts.append(jnp.concatenate(
            [rest[:, :LANES // 2], rest[:snaps - 16, LANES // 2:]], axis=0))
    return jnp.concatenate(parts, axis=1)


def packed_rows(snaps, columns):
    return columns // LANES * snaps + (16 if columns % LANES else 0)


def kernel(n, fold, tiles_hbm, dirs_hbm, cols_hbm, counts_hbm, weights_hbm, out_ref,
           dirs_ref, cols_ref, counts_ref, weights_ref, tiles, dirs,
           snap_out, snap_own, snap_far, gram_own, gram_far, own_out, own_in, far_out, far_in,
           arg_sem, tile_sem, own_send1, own_recv1, far_send1, far_recv1,
           own_send2, own_recv2, far_send2, far_recv2):
    me = lax.axis_index("member")
    per_row, row_tiles = cols_ref.shape
    snaps = dirs_ref.shape[1]
    chunk = row_tiles // n
    each = chunk // fold
    half = n // 2
    side, loc = me // half, me % half
    mine, other = side * half, (1 - side) * half
    rows_half = half * snaps
    mid = half // 2

    def nth(step):
        off = mid + (step % 2) * ((step + 1) // 2) - ((step + 1) % 2) * (step // 2)
        return lax.rem(loc + off, half)

    def slab_start(spot, which):
        return (2 * spot + (side if which == 0 else 1 - side)) * chunk

    def tile_copy(step, which):
        rows = pl.ds(slab_start(nth(step), which), chunk)
        return pltpu.make_async_copy(
            tiles_hbm.at[0, rows], tiles.at[rows], tile_sem.at[which, step])

    def remote(src, dst, send, recv, dest):
        return pltpu.make_async_remote_copy(
            src_ref=src, dst_ref=dst, send_sem=send, recv_sem=recv,
            device_id={"member": dest}, device_id_type=MESH)

    def own_snap(spot, source):
        return remote(snap_out.at[spot], snap_own.at[source], own_send1.at[spot],
                      own_recv1.at[source], mine + spot)

    def far_snap(spot, source):
        return remote(snap_out.at[spot, 1], snap_far.at[source], far_send1.at[spot],
                      far_recv1.at[source], other + spot)

    def own_gram(spot, source):
        return remote(own_out.at[spot], own_in.at[source], own_send2.at[spot],
                      own_recv2.at[source], mine + spot)

    def far_gram(spot, source):
        return remote(far_out.at[spot], far_in.at[source], far_send2.at[spot],
                      far_recv2.at[source], other + spot)

    args = [
        pltpu.make_async_copy(a, b, arg_sem.at[i]) for i, (a, b) in enumerate(
            [(dirs_hbm, dirs_ref), (cols_hbm, cols_ref), (counts_hbm, counts_ref),
             (weights_hbm, weights_ref)])
    ]
    for copy in args:
        copy.start()

    def start_tiles(step, carry):
        tile_copy(step, 1).start()
        tile_copy(step, 0).start()
        return carry

    lax.fori_loop(0, half, start_tiles, 0)

    barrier = pltpu.get_barrier_semaphore()

    def greet(off, carry):
        pl.semaphore_signal(barrier, inc=1, device_id={"member": lax.rem(me + off, n)},
                            device_id_type=MESH)
        return carry

    lax.fori_loop(1, n, greet, 0)

    for copy in args:
        copy.wait()
    for c in range(row_tiles):
        dirs[c] = dirs_ref[0, :, c * LANES:(c + 1) * LANES]
    dirs[row_tiles] = jnp.zeros(dirs.shape[1:], dirs.dtype)

    def product(spot, which):
        parts = []
        for t in range(chunk):
            r = slab_start(spot, which) + t
            picked = [dirs[jnp.where(k < counts_ref[r], cols_ref[k, r], row_tiles)]
                      for k in range(per_row)]
            lhs = jnp.concatenate(picked, axis=1)
            rhs = jnp.concatenate([tiles[r, k] for k in range(per_row)], axis=1)
            parts.append(lax.dot_general(lhs, rhs, (((1,), (1,)), ((), ())),
                                         preferred_element_type=jnp.float32))
        rows = [jnp.concatenate(parts[f * each:(f + 1) * each], axis=1) for f in range(fold)]
        return jnp.concatenate(rows, axis=0).astype(jnp.bfloat16)

    first = nth(0)
    tile_copy(0, 1).wait()
    snap_out[first, 1] = product(first, 1)
    pl.semaphore_wait(barrier, n - 1)
    far_snap(first, loc).start()
    tile_copy(0, 0).wait()
    snap_out[first, 0] = product(first, 0)
    own_snap(first, loc).start()

    def body(step, carry):
        spot = nth(step)
        tile_copy(step, 1).wait()
        snap_out[spot, 1] = product(spot, 1)
        far_snap(spot, loc).start()
        tile_copy(step, 0).wait()
        snap_out[spot, 0] = product(spot, 0)
        own_snap(spot, loc).start()
        return carry

    lax.fori_loop(1, half - 1, body, 0)
    tile_copy(half - 1, 1).wait()
    last = product(loc, 1)
    snap_out[loc, 1] = last
    far_snap(loc, loc).start()
    snap_own[loc, 1] = last
    tile_copy(half - 1, 0).wait()
    snap_own[loc, 0] = product(loc, 0)

    def land(step, carry):
        own_snap(loc, nth(step)).wait_recv()
        far_snap(loc, nth(step)).wait_recv()
        return carry

    lax.fori_loop(0, half - 1, land, 0)
    far_snap(loc, loc).wait_recv()

    def operands(read, which):
        flats, weighteds = [], []
        for f in range(fold):
            for t in range(each):
                got = read(t).astype(jnp.float32)
                flat = got[:, f * snaps:(f + 1) * snaps].reshape(rows_half, LANES)
                w = weights_ref[pl.ds(slab_start(loc, which) + f * each + t, 1), :]
                flats.append(flat.astype(jnp.bfloat16))
                weighteds.append((flat * w).astype(jnp.bfloat16))
        return flats, weighteds

    flat0, weighted0 = operands(lambda t: snap_own[:, 0, :, t * LANES:(t + 1) * LANES], 0)
    flat1, weighted1 = operands(lambda t: snap_own[:, 1, :, t * LANES:(t + 1) * LANES], 1)
    flat2, weighted2 = operands(lambda t: snap_far[:, :, t * LANES:(t + 1) * LANES], 0)

    def outer(left, right):
        return lax.dot_general(
            jnp.concatenate(left, axis=1), jnp.concatenate(right, axis=1),
            (((1,), (1,)), ((), ())), preferred_element_type=jnp.float32)

    gram_far[...] = outer(weighted2, flat0).reshape(half, snaps, rows_half)

    def give_far(step, carry):
        spot = nth(step)
        far_out[spot] = pack(gram_far[spot]).astype(jnp.bfloat16)
        far_gram(spot, loc).start()
        return carry

    lax.fori_loop(0, half, give_far, 0)
    gram_own[0] = outer(weighted0 + weighted1, flat0 + flat1).reshape(half, snaps, rows_half)
    gram_own[1] = outer(weighted0, flat2).reshape(half, snaps, rows_half)

    def give_own(step, carry):
        spot = nth(step)
        both = jnp.concatenate([gram_own[0, spot], gram_own[1, spot]], axis=1)
        own_out[spot] = pack(both).astype(jnp.bfloat16)
        own_gram(spot, loc).start()
        return carry

    lax.fori_loop(0, half - 1, give_own, 0)
    both = jnp.concatenate([gram_own[0, loc], gram_own[1, loc]], axis=1)
    own_sum = pack(both)

    def take_own(step, total):
        source = nth(step)
        own_gram(loc, source).wait_recv()
        return total + own_in[source].astype(jnp.float32)

    own_sum = lax.fori_loop(0, half - 1, take_own, own_sum)

    def take_far(step, total):
        source = nth(step)
        far_gram(loc, source).wait_recv()
        return total + far_in[source].astype(jnp.float32)

    far_sum = lax.fori_loop(
        0, half, take_far, jnp.zeros(far_in.shape[1:], jnp.float32))
    own = unpack(own_sum, snaps, 2 * rows_half)
    near = own[:, :rows_half]
    far = own[:, rows_half:] + unpack(far_sum, snaps, rows_half)
    out_ref[...] = jnp.where(side == 0, jnp.concatenate([near, far], axis=1),
                             jnp.concatenate([far, near], axis=1))

    def drain(step, carry):
        spot = nth(step)
        own_snap(spot, loc).wait_send()
        own_gram(spot, loc).wait_send()
        far_snap(spot, loc).wait_send()
        far_gram(spot, loc).wait_send()
        return carry

    lax.fori_loop(0, half - 1, drain, 0)
    far_snap(loc, loc).wait_send()
    far_gram(loc, loc).wait_send()


def per_device(n, tile_values, directions, columns, counts, weights):
    _, row_tiles, per_row, size, _ = tile_values.shape
    snaps = directions.shape[1]
    chunk = row_tiles // n
    half = n // 2
    fold = 2 if chunk % 2 == 0 else 1
    slab = (fold * snaps, chunk * size // fold)
    own_rows = packed_rows(snaps, n * snaps)
    far_rows = packed_rows(snaps, half * snaps)
    hbm = pl.BlockSpec(memory_space=pltpu.HBM)
    dma = pltpu.SemaphoreType.DMA
    return pl.pallas_call(
        functools.partial(kernel, n, fold),
        out_shape=jax.ShapeDtypeStruct((snaps, n * snaps), jnp.float32),
        in_specs=[hbm] * 5,
        out_specs=pl.BlockSpec(memory_space=pltpu.VMEM),
        scratch_shapes=[
            pltpu.VMEM(directions.shape, jnp.bfloat16),
            pltpu.SMEM((per_row, row_tiles), jnp.int32),
            pltpu.SMEM((row_tiles,), jnp.int32),
            pltpu.VMEM((row_tiles, size), jnp.float32),
            pltpu.VMEM((row_tiles, per_row, size, size), jnp.bfloat16),
            pltpu.VMEM((row_tiles + 1, snaps, size), jnp.bfloat16),
            pltpu.VMEM((half, 2, *slab), jnp.bfloat16),
            pltpu.VMEM((half, 2, *slab), jnp.bfloat16),
            pltpu.VMEM((half, *slab), jnp.bfloat16),
            pltpu.VMEM((2, half, snaps, half * snaps), jnp.float32),
            pltpu.VMEM((half, snaps, half * snaps), jnp.float32),
            pltpu.VMEM((half, own_rows, LANES), jnp.bfloat16),
            pltpu.VMEM((half, own_rows, LANES), jnp.bfloat16),
            pltpu.VMEM((half, far_rows, LANES), jnp.bfloat16),
            pltpu.VMEM((half, far_rows, LANES), jnp.bfloat16),
            dma((4,)), dma((2, half)),
            *[dma((half,)) for _ in range(8)],
        ],
        compiler_params=pltpu.CompilerParams(
            collective_id=0, has_side_effects=True, vmem_limit_bytes=64 * 2**20),
    )(tile_values, directions, columns.T, counts, weights.reshape(-1, LANES))


def solution(mesh):
    in_specs = (
        P(("groups", "member"), None, None, None, None),
        P(("groups", "member"), None, None),
        P(),
        P(),
        P(),
    )
    out_specs = P(("groups", "member"), None)
    return jax.shard_map(
        functools.partial(per_device, mesh.shape["member"]), mesh=mesh,
        in_specs=in_specs, out_specs=out_specs, check_vma=False
    )
```

```python
import functools

import jax
import jax.numpy as jnp
from jax import lax
from jax.experimental import pallas as pl
from jax.experimental.pallas import tpu as pltpu
from jax.sharding import PartitionSpec as P

MESH = pl.DeviceIdType.MESH
LANES = 128


def pack(block):
    snaps, columns = block.shape
    full = columns // LANES
    rows = [block[:, c * LANES:(c + 1) * LANES] for c in range(full)]
    if columns % LANES:
        rest = block[:, full * LANES:]
        left = rest[:16]
        right = jnp.concatenate([rest[16:], jnp.zeros((32 - snaps, LANES // 2), rest.dtype)], axis=0)
        rows.append(jnp.concatenate([left, right], axis=1))
    return jnp.concatenate(rows, axis=0)


def unpack(rows, snaps, columns):
    full = columns // LANES
    parts = [rows[c * snaps:(c + 1) * snaps] for c in range(full)]
    if columns % LANES:
        rest = rows[full * snaps:]
        parts.append(jnp.concatenate(
            [rest[:, :LANES // 2], rest[:snaps - 16, LANES // 2:]], axis=0))
    return jnp.concatenate(parts, axis=1)


def packed_rows(snaps, columns):
    return columns // LANES * snaps + (16 if columns % LANES else 0)


def kernel(n, fold, tiles_hbm, dirs_hbm, cols_hbm, counts_hbm, weights_hbm, out_ref,
           dirs_ref, cols_ref, counts_ref, weights_ref, tiles, dirs,
           snap_out, snap_own, snap_far, gram_near, gram_far, near_out, near_in,
           cross_out, cross_in, far_out, far_in,
           arg_sem, tile_sem, own_send1, own_recv1, far_send1, far_recv1,
           near_send, near_recv, cross_send, cross_recv, far_send2, far_recv2):
    me = lax.axis_index("member")
    per_row, row_tiles = cols_ref.shape
    snaps = dirs_ref.shape[1]
    chunk = row_tiles // n
    each = chunk // fold
    half = n // 2
    side, loc = me // half, me % half
    mine, other = side * half, (1 - side) * half
    rows_half = half * snaps
    mid = half // 2

    def nth(step):
        off = mid + (step % 2) * ((step + 1) // 2) - ((step + 1) % 2) * (step // 2)
        return lax.rem(loc + off, half)

    def slab_start(spot, which):
        return (2 * spot + (side if which == 0 else 1 - side)) * chunk

    def tile_copy(step, which):
        rows = pl.ds(slab_start(nth(step), which), chunk)
        return pltpu.make_async_copy(
            tiles_hbm.at[0, rows], tiles.at[rows], tile_sem.at[which, step])

    def remote(src, dst, send, recv, dest):
        return pltpu.make_async_remote_copy(
            src_ref=src, dst_ref=dst, send_sem=send, recv_sem=recv,
            device_id={"member": dest}, device_id_type=MESH)

    def own_snap(spot, source):
        return remote(snap_out.at[spot], snap_own.at[source], own_send1.at[spot],
                      own_recv1.at[source], mine + spot)

    def far_snap(spot, source):
        return remote(snap_out.at[spot, 1], snap_far.at[source], far_send1.at[spot],
                      far_recv1.at[source], other + spot)

    def near_sum(spot, source):
        return remote(near_out.at[spot], near_in.at[source], near_send.at[spot],
                      near_recv.at[source], mine + spot)

    def cross_sum(spot, source):
        return remote(cross_out.at[spot], cross_in.at[source], cross_send.at[spot],
                      cross_recv.at[source], mine + spot)

    def far_sum(spot, source):
        return remote(far_out.at[spot], far_in.at[source], far_send2.at[spot],
                      far_recv2.at[source], other + spot)

    args = [
        pltpu.make_async_copy(a, b, arg_sem.at[i]) for i, (a, b) in enumerate(
            [(dirs_hbm, dirs_ref), (cols_hbm, cols_ref), (counts_hbm, counts_ref),
             (weights_hbm, weights_ref)])
    ]
    for copy in args:
        copy.start()

    def start_tiles(step, carry):
        tile_copy(step, 1).start()
        tile_copy(step, 0).start()
        return carry

    lax.fori_loop(0, half, start_tiles, 0)

    barrier = pltpu.get_barrier_semaphore()

    def greet(off, carry):
        pl.semaphore_signal(barrier, inc=1, device_id={"member": lax.rem(me + off, n)},
                            device_id_type=MESH)
        return carry

    lax.fori_loop(1, n, greet, 0)

    for copy in args:
        copy.wait()
    for c in range(row_tiles):
        dirs[c] = dirs_ref[0, :, c * LANES:(c + 1) * LANES]
    dirs[row_tiles] = jnp.zeros(dirs.shape[1:], dirs.dtype)

    def product(spot, which):
        parts = []
        for t in range(chunk):
            r = slab_start(spot, which) + t
            picked = [dirs[jnp.where(k < counts_ref[r], cols_ref[k, r], row_tiles)]
                      for k in range(per_row)]
            lhs = jnp.concatenate(picked, axis=1)
            rhs = jnp.concatenate([tiles[r, k] for k in range(per_row)], axis=1)
            parts.append(lax.dot_general(lhs, rhs, (((1,), (1,)), ((), ())),
                                         preferred_element_type=jnp.float32))
        rows = [jnp.concatenate(parts[f * each:(f + 1) * each], axis=1) for f in range(fold)]
        return jnp.concatenate(rows, axis=0).astype(jnp.bfloat16)

    first = nth(0)
    tile_copy(0, 1).wait()
    snap_out[first, 1] = product(first, 1)
    pl.semaphore_wait(barrier, n - 1)
    far_snap(first, loc).start()
    tile_copy(0, 0).wait()
    snap_out[first, 0] = product(first, 0)
    own_snap(first, loc).start()

    def body(step, carry):
        spot = nth(step)
        tile_copy(step, 1).wait()
        snap_out[spot, 1] = product(spot, 1)
        far_snap(spot, loc).start()
        tile_copy(step, 0).wait()
        snap_out[spot, 0] = product(spot, 0)
        own_snap(spot, loc).start()
        return carry

    lax.fori_loop(1, half - 1, body, 0)
    tile_copy(half - 1, 1).wait()
    last = product(loc, 1)
    snap_out[loc, 1] = last
    far_snap(loc, loc).start()
    snap_own[loc, 1] = last
    tile_copy(half - 1, 0).wait()
    snap_own[loc, 0] = product(loc, 0)

    def land_own(step, carry):
        own_snap(loc, nth(step)).wait_recv()
        return carry

    lax.fori_loop(0, half - 1, land_own, 0)

    def operands(read, which):
        flats, weighteds = [], []
        for f in range(fold):
            for t in range(each):
                got = read(t).astype(jnp.float32)
                flat = got[:, f * snaps:(f + 1) * snaps].reshape(rows_half, LANES)
                w = weights_ref[pl.ds(slab_start(loc, which) + f * each + t, 1), :]
                flats.append(flat.astype(jnp.bfloat16))
                weighteds.append((flat * w).astype(jnp.bfloat16))
        return flats, weighteds

    flat0, weighted0 = operands(lambda t: snap_own[:, 0, :, t * LANES:(t + 1) * LANES], 0)
    flat1, weighted1 = operands(lambda t: snap_own[:, 1, :, t * LANES:(t + 1) * LANES], 1)
    def outer(left, right):
        return lax.dot_general(
            jnp.concatenate(left, axis=1), jnp.concatenate(right, axis=1),
            (((1,), (1,)), ((), ())), preferred_element_type=jnp.float32)

    def give(gram, out, copy, steps):
        def send(step, carry):
            spot = nth(step)
            out[spot] = pack(gram[spot]).astype(out.dtype)
            copy(spot, loc).start()
            return carry

        lax.fori_loop(0, steps, send, 0)
        return pack(gram[loc])

    def take(arrived, copy, steps, total):
        def add(step, total):
            source = nth(step)
            copy(loc, source).wait_recv()
            return total + arrived[source].astype(jnp.float32)

        return lax.fori_loop(0, steps, add, total)

    gram_near[...] = outer(weighted0 + weighted1, flat0 + flat1).reshape(gram_near.shape)
    near = give(gram_near, near_out, near_sum, half - 1)

    def land_far(step, carry):
        far_snap(loc, nth(step)).wait_recv()
        return carry

    lax.fori_loop(0, half, land_far, 0)
    flat2, weighted2 = operands(lambda t: snap_far[:, :, t * LANES:(t + 1) * LANES], 0)

    gram_far[...] = outer(weighted2, flat0).reshape(gram_far.shape)
    give(gram_far, far_out, far_sum, half)
    gram_far[...] = outer(weighted0, flat2).reshape(gram_far.shape)
    cross = give(gram_far, cross_out, cross_sum, half - 1)

    near = unpack(take(near_in, near_sum, half - 1, near), snaps, rows_half)
    cross = take(cross_in, cross_sum, half - 1, cross)
    cross = unpack(take(far_in, far_sum, half, cross), snaps, rows_half)
    out_ref[...] = jnp.where(side == 0, jnp.concatenate([near, cross], axis=1),
                             jnp.concatenate([cross, near], axis=1))

    def drain(step, carry):
        spot = nth(step)
        own_snap(spot, loc).wait_send()
        far_snap(spot, loc).wait_send()
        near_sum(spot, loc).wait_send()
        cross_sum(spot, loc).wait_send()
        far_sum(spot, loc).wait_send()
        return carry

    lax.fori_loop(0, half - 1, drain, 0)
    far_snap(loc, loc).wait_send()
    far_sum(loc, loc).wait_send()


def per_device(n, tile_values, directions, columns, counts, weights):
    _, row_tiles, per_row, size, _ = tile_values.shape
    snaps = directions.shape[1]
    chunk = row_tiles // n
    half = n // 2
    fold = 2 if chunk % 2 == 0 else 1
    slab = (fold * snaps, chunk * size // fold)
    block = (packed_rows(snaps, half * snaps), LANES)
    hbm = pl.BlockSpec(memory_space=pltpu.HBM)
    dma = pltpu.SemaphoreType.DMA
    return pl.pallas_call(
        functools.partial(kernel, n, fold),
        out_shape=jax.ShapeDtypeStruct((snaps, n * snaps), jnp.float32),
        in_specs=[hbm] * 5,
        out_specs=pl.BlockSpec(memory_space=pltpu.VMEM),
        scratch_shapes=[
            pltpu.VMEM(directions.shape, jnp.bfloat16),
            pltpu.SMEM((per_row, row_tiles), jnp.int32),
            pltpu.SMEM((row_tiles,), jnp.int32),
            pltpu.VMEM((row_tiles, size), jnp.float32),
            pltpu.VMEM((row_tiles, per_row, size, size), jnp.bfloat16),
            pltpu.VMEM((row_tiles + 1, snaps, size), jnp.bfloat16),
            pltpu.VMEM((half, 2, *slab), jnp.bfloat16),
            pltpu.VMEM((half, 2, *slab), jnp.bfloat16),
            pltpu.VMEM((half, *slab), jnp.bfloat16),
            pltpu.VMEM((half, snaps, half * snaps), jnp.float32),
            pltpu.VMEM((half, snaps, half * snaps), jnp.float32),
            pltpu.VMEM((half, *block), jnp.bfloat16),
            pltpu.VMEM((half, *block), jnp.bfloat16),
            pltpu.VMEM((half, *block), jnp.bfloat16),
            pltpu.VMEM((half, *block), jnp.bfloat16),
            pltpu.VMEM((half, *block), jnp.bfloat16),
            pltpu.VMEM((half, *block), jnp.bfloat16),
            dma((4,)), dma((2, half)),
            *[dma((half,)) for _ in range(10)],
        ],
        compiler_params=pltpu.CompilerParams(
            collective_id=0, has_side_effects=True, vmem_limit_bytes=64 * 2**20),
    )(tile_values, directions, columns.T, counts, weights.reshape(-1, LANES))


def solution(mesh):
    in_specs = (
        P(("groups", "member"), None, None, None, None),
        P(("groups", "member"), None, None),
        P(),
        P(),
        P(),
    )
    out_specs = P(("groups", "member"), None)
    return jax.shard_map(
        functools.partial(per_device, mesh.shape["member"]), mesh=mesh,
        in_specs=in_specs, out_specs=out_specs, check_vma=False
    )
```
